256 devices in a mesh: dp: 2 (over z_lo), col: 16 (over y, z_hi), red: 8 (over x, core).
Axes of the slice: x: 4, y: 4, z: 8 (z_hi: 4, z_lo: 2; z = z_hi * 2 + z_lo), core: 2. Of those that a mesh axis runs over, the one named last changes fastest.
Arguments:
- inputs: bfloat16 [1024, 8192], P(('dp', 'col'), 'red'), may hold values from -6 to 6
- out_grad: bfloat16 [1024, 8192], P(('dp', 'col'), 'red'), may hold values from -1.5 to 1.5
- w_gate: bfloat16 [8192, 14336], P('red', 'col'), may hold values from -0.125 to 0.125
- w_up: bfloat16 [8192, 14336], P('red', 'col'), may hold values from -0.125 to 0.125
- w_down: bfloat16 [14336, 8192], P('col', 'red'), may hold values from -0.09375 to 0.09375
- block_mask: int32 [64, 112], P('red', 'col'), may hold values 0 or 1
Outputs:
- output: bfloat16 [1024, 8192], P(('dp', 'col'), 'red')
- input_grad: bfloat16 [1024, 8192], P(('dp', 'col'), 'red')
- grad_gate: bfloat16 [8192, 14336], P('red', 'col')
- grad_up: bfloat16 [8192, 14336], P('red', 'col')
- grad_down: bfloat16 [14336, 8192], P('col', 'red')
The draws below stay inside these ranges and needn't reach their ends.
All inputs are finite; a program needn't handle non-finite values. No bound on the sum of `block_mask` on one device may be relied on, other than what follows from the above.
Results may differ from the reference program's by a relative error of at most 0.005.
Values may be sent and summed in bfloat16 or wider, within the bound.
No kernel may reach another device: no remote copies, remote signals or barrier semaphores. Data moves between devices by JAX's collectives and lax.ppermute only.
A program may use at most 128 MiB of HBM per device.

```python
import jax
import jax.numpy as jnp

D = 8192
FF = 14336
BLK = 128
TOKENS = 1024
DB = 64
FB = 112


def touch_ends(array, key, least, top_value):
    spot = [jax.random.randint(jax.random.fold_in(key, axis), (), 0, length) for axis, length in enumerate(array.shape)]
    longest = array.shape.index(max(array.shape))
    neighbour = spot[:longest] + [(spot[longest] + 1) % array.shape[longest]] + spot[longest + 1:]
    return array.at[tuple(spot)].set(least).at[tuple(neighbour)].set(top_value)


def shard_levels(own_key, extent, pieces, least, top_value):
    level, own = 1.0, jax.random.fold_in(own_key, 6)
    for axis_at, shards_of in pieces:
        draws = jnp.exp(jax.random.uniform(jax.random.fold_in(own, axis_at), (shards_of,), jnp.float32, least / len(pieces), top_value / len(pieces)))
        level = level * jnp.repeat(draws, extent[axis_at] // shards_of).reshape([-1 if axis == axis_at else 1 for axis in range(len(extent))])
    return level


def gaussian(key, extent, scale, reach, pieces=(), kind=jnp.bfloat16):
    drawn = scale * jax.random.normal(key, extent, jnp.float32)
    if pieces:
        drawn = drawn * shard_levels(key, extent, pieces, -0.22, 0.18)
    return jnp.clip(drawn, -reach, reach).astype(kind)


def setup_inputs(seed: int = 0) -> dict:
    seeds = jax.random.split(jax.random.key(seed), 7)
    return {
        "inputs": gaussian(seeds[0], (TOKENS, D), 1.0, 6.0, ((0, 32), (1, 8))),
        "out_grad": gaussian(seeds[1], (TOKENS, D), 0.25, 1.5, ((0, 32), (1, 8))),
        "w_gate": gaussian(seeds[2], (D, FF), (D // 4) ** -0.5, 0.125, ((0, 8), (1, 16))),
        "w_up": gaussian(seeds[3], (D, FF), (D // 4) ** -0.5, 0.125, ((0, 8), (1, 16))),
        "w_down": gaussian(seeds[4], (FF, D), (FF // 4) ** -0.5, 0.09375, ((0, 16), (1, 8))),
        "block_mask": touch_ends((jax.random.randint(seeds[5], (DB, FB), 0, 4) < 1).astype(jnp.int32), jax.random.fold_in(seeds[5], 1), 0, 1),
    }


def spread_mask(block_mask, block_size):
    return jnp.repeat(jnp.repeat(block_mask, block_size, axis=0), block_size, axis=1).astype(jnp.bfloat16)


def reference(inputs, out_grad, w_gate, w_up, w_down, block_mask):
    element_mask = spread_mask(block_mask, BLK)
    gate_eff = w_gate * element_mask
    up_eff = w_up * element_mask
    down_eff = w_down * element_mask.T
    gate_pre = jnp.dot(inputs, gate_eff, preferred_element_type=jnp.float32)
    up_pre = jnp.dot(inputs, up_eff, preferred_element_type=jnp.float32)
    sigmoid_gate = jax.nn.sigmoid(gate_pre)
    hidden = (gate_pre * sigmoid_gate * up_pre).astype(jnp.bfloat16)
    output = jnp.dot(hidden, down_eff, preferred_element_type=jnp.float32).astype(jnp.bfloat16)
    hidden_grad = jnp.dot(out_grad, down_eff.T, preferred_element_type=jnp.float32)
    gate_grad = (hidden_grad * up_pre * sigmoid_gate * (1.0 + gate_pre * (1.0 - sigmoid_gate))).astype(jnp.bfloat16)
    up_grad = (hidden_grad * gate_pre * sigmoid_gate).astype(jnp.bfloat16)
    input_grad = (jnp.dot(gate_grad, gate_eff.T, preferred_element_type=jnp.float32)
                  + jnp.dot(up_grad, up_eff.T, preferred_element_type=jnp.float32)).astype(jnp.bfloat16)
    grad_gate = (jnp.dot(inputs.T, gate_grad, preferred_element_type=jnp.float32) * element_mask).astype(jnp.bfloat16)
    grad_up = (jnp.dot(inputs.T, up_grad, preferred_element_type=jnp.float32) * element_mask).astype(jnp.bfloat16)
    grad_down = (jnp.dot(hidden.T, out_grad, preferred_element_type=jnp.float32) * element_mask.T).astype(jnp.bfloat16)
    return output, input_grad, grad_gate, grad_up, grad_down
```

```python
import jax
import jax.numpy as jnp
from jax import lax
from jax.sharding import Mesh, PartitionSpec as P

BLK = 128
F32 = jnp.float32
BF16 = jnp.bfloat16

ROWS = (((1,), (1,)), ((), ()))
COLS = (((0,), (0,)), ((), ()))


def shift(value, axis, step, size):
    return lax.ppermute(value, axis, [(i, (i + step) % size) for i in range(size)])


def swap(value, axis):
    return lax.ppermute(value, axis, [(0, 1), (1, 0)])


def gather_ring(own, axis):
    half = own.shape[0] // 2
    before = shift(own, axis, 1, 4)
    after = shift(own, axis, -1, 4)
    far = jnp.concatenate([shift(before[:half], axis, 1, 4), shift(after[half:], axis, -1, 4)], axis=0)
    return [own, after, far, before]


def scatter_ring(chunks):
    def run(axis, parts):
        half = parts[0].shape[0] // 2
        ahead = shift(parts[2][:half].astype(BF16), axis, 1, 4)
        behind = shift(parts[2][half:].astype(BF16), axis, -1, 4)
        forward = jnp.concatenate([parts[1][:half] + ahead.astype(F32), parts[1][half:]], axis=0)
        backward = jnp.concatenate([parts[3][:half], parts[3][half:] + behind.astype(F32)], axis=0)
        first = shift(forward.astype(BF16), axis, 1, 4)
        second = shift(backward.astype(BF16), axis, -1, 4)
        return parts[0] + first.astype(F32) + second.astype(F32)

    return run(*chunks)


def scatter_direct(axis, parts):
    got = [shift(parts[k].astype(BF16), axis, k, 4) for k in (1, 2, 3)]
    return parts[0] + (got[0].astype(F32) + got[1].astype(F32) + got[2].astype(F32))


def turn(value, start, axis):
    size = value.shape[axis]
    return lax.dynamic_slice_in_dim(jnp.concatenate([value, value], axis=axis), start, size, axis=axis)


def local(inputs, out_grad, w_gate, w_up, w_down, block_mask):
    rows, feats = inputs.shape
    hid = w_gate.shape[1]
    quad = rows // 8
    x = lax.axis_index("x")
    core = lax.axis_index("core")

    element_mask = jnp.repeat(jnp.repeat(block_mask, BLK, axis=0), BLK, axis=1).astype(BF16)
    gate_eff = w_gate * element_mask
    up_eff = w_up * element_mask
    down_eff = w_down * element_mask.T
    joined = jnp.concatenate([gate_eff, up_eff], axis=1)

    def own_rows(value):
        return turn(turn(value.reshape(4, 2, quad, feats), x, 0), core, 1).reshape(8, quad, feats)

    def gather_z(value):
        return jnp.concatenate(gather_ring(value, "zh"), axis=1)

    def gather_y(value):
        return jnp.concatenate(gather_ring(value, "y"), axis=1).reshape(16 * rows, feats)

    tok_z = gather_z(own_rows(inputs))
    cot_z = gather_z(own_rows(out_grad))
    tokens = gather_y(tok_z)
    cotangent = gather_y(cot_z)
    other_z = swap(jnp.stack([tok_z, cot_z]), "dp")
    other_tokens = gather_y(other_z[0])
    other_cot = gather_y(other_z[1])

    def sum_red(partial):
        width = partial.shape[1]
        split = partial.reshape(4, 2, -1, width)
        both = split[:, 0] + swap(split[:, 1].astype(BF16), "core").astype(F32)
        return scatter_ring(("x", [both[k] for k in range(4)]))

    pre = sum_red(jnp.dot(tokens, joined, preferred_element_type=F32))
    gate_pre, up_pre = pre[:, :hid], pre[:, hid:]
    sig = jax.nn.sigmoid(gate_pre)
    hidden = (gate_pre * sig * up_pre).astype(BF16)

    hidden_grad = sum_red(lax.dot_general(cotangent, down_eff, ROWS, preferred_element_type=F32))
    gate_grad = (hidden_grad * up_pre * sig * (1.0 + gate_pre * (1.0 - sig))).astype(BF16)
    up_grad = (hidden_grad * gate_pre * sig).astype(BF16)
    grads = jnp.concatenate([gate_grad, up_grad], axis=1)

    def gather_red(value):
        mine = jnp.stack(gather_ring(value, "x"))
        both = jnp.stack([mine, swap(mine, "core")], axis=1)
        return both.reshape(-1, value.shape[1])

    hidden_all = gather_red(hidden)
    grads_all = gather_red(grads)
    other_acts = gather_red(swap(jnp.concatenate([hidden, grads], axis=1), "dp"))
    other_hidden = other_acts[:, :hid]
    other_grads = other_acts[:, hid:]

    def sum_col(partial):
        parts = partial.reshape(8, 4, 4 * quad, feats)
        mine = scatter_ring(("y", [parts[:, k] for k in range(4)]))
        parts = mine.reshape(8, 4, quad, feats)
        mine = scatter_direct("zh", [parts[:, k] for k in range(4)])
        return turn(turn(mine.reshape(4, 2, quad, feats), (4 - x) % 4, 0), core, 1).reshape(rows, feats).astype(BF16)

    output = sum_col(jnp.dot(hidden_all, down_eff, preferred_element_type=F32))
    input_grad = sum_col(lax.dot_general(grads_all, joined, ROWS, preferred_element_type=F32))

    def weight_grad(a, b, other_a, other_b):
        return lax.dot_general(a, b, COLS, preferred_element_type=F32) + lax.dot_general(
            other_a, other_b, COLS, preferred_element_type=F32
        )

    grad_down = (weight_grad(hidden_all, cotangent, other_hidden, other_cot) * element_mask.T).astype(BF16)
    grad_gate = (
        weight_grad(tokens, grads_all[:, :hid], other_tokens, other_grads[:, :hid]) * element_mask
    ).astype(BF16)
    grad_up = (
        weight_grad(tokens, grads_all[:, hid:], other_tokens, other_grads[:, hid:]) * element_mask
    ).astype(BF16)
    return output, input_grad, grad_gate, grad_up, grad_down


def solution(mesh):
    split = Mesh(mesh.devices.reshape(2, 4, 4, 4, 2), ("dp", "y", "zh", "x", "core"))
    token_rows = P(("dp", "y", "zh"), ("x", "core"))
    weight_in = P(("x", "core"), ("y", "zh"))
    weight_out = P(("y", "zh"), ("x", "core"))
    return jax.shard_map(
        local,
        mesh=split,
        in_specs=(token_rows, token_rows, weight_in, weight_in, weight_out, weight_in),
        out_specs=(token_rows, token_rows, weight_in, weight_in, weight_out),
        check_vma=False,
    )
```

```python
import jax
import jax.numpy as jnp
from jax import lax
from jax.experimental import pallas as pl
from jax.experimental.pallas import tpu as pltpu
from jax.sharding import Mesh, PartitionSpec as P

BLK = 128
F32 = jnp.float32
BF16 = jnp.bfloat16

ROWS = (((1,), (1,)), ((), ()))
COLS = (((0,), (0,)), ((), ()))

PARTNERS = ((1, 3), (3, 1))


def exchange(value, axis, step):
    pairs = [(2 * i + c, 2 * (i ^ PARTNERS[c][step]) + c) for i in range(4) for c in range(2)]
    return lax.ppermute(value, (axis, "core"), pairs)


def swap(value, axis):
    return lax.ppermute(value, axis, [(0, 1), (1, 0)])


def after(value, *earlier):
    return lax.optimization_barrier((value, *earlier))[0]


def whole(shape):
    return pl.BlockSpec(shape, lambda j: (0,) * len(shape), pipeline_mode=pl.Buffered(1))


def scalars():
    return pl.BlockSpec(memory_space=pltpu.SMEM)


def keep(flag, block):
    return jnp.where(flag > 0, block, jnp.zeros_like(block))


def row_pieces(first, own, near, rest):
    size = own.shape[0]
    other = rest[:size, :]
    return [own[...], jnp.where(first, near[...], other), jnp.where(first, other, near[...]), rest[size:, :]]


def acts_rows(side, two, rest, two_swapped, rest_swapped):
    pieces = [(two, two_swapped, 0), (two, two_swapped, 1), (rest, rest_swapped, 0), (rest, rest_swapped, 1)]
    return jnp.concatenate(
        [ref[k, side, y] for y in range(4) for mine, sibling, k in pieces for ref in (mine, sibling)], axis=0
    )


def forward_kernel(core, mask, own, near, rest, wg, wu, wd, kept, sent, rows):
    j = pl.program_id(0)
    feats = wg.shape[0]
    blocks = feats // BLK

    @pl.when(j == 0)
    def _():
        rows[...] = jnp.concatenate(row_pieces(core[0] == 0, own, near, rest), axis=0)

    gate_up = jnp.concatenate(
        [
            jnp.concatenate([keep(mask[k, j], w[k * BLK : (k + 1) * BLK, :]) for k in range(blocks)], axis=0)
            for w in (wg, wu)
        ],
        axis=1,
    )
    down = jnp.concatenate([keep(mask[k, j], wd[:, k * BLK : (k + 1) * BLK]) for k in range(blocks)], axis=1)
    pre = jnp.dot(rows[:, :feats], gate_up, preferred_element_type=F32)
    back = lax.dot_general(rows[:, feats:], down, ROWS, preferred_element_type=F32)
    for side, acc in enumerate((pre[:, :BLK], pre[:, BLK:], back)):
        acc = acc.reshape(4, 4, 2, acc.shape[0] // 32, BLK)
        for k in range(4):
            kept[k, side] = acc[:, k, 0]
            sent[k, side] = acc[:, k, 1]


def forward(core, mask, own, near, rest, w_gate, w_up, w_down):
    feats, hid = w_gate.shape
    tok = 4 * own.shape[0]
    shape = jax.ShapeDtypeStruct((4, 3, 4, tok // 32, hid), F32)
    out = pl.BlockSpec((4, 3, 4, tok // 32, BLK), lambda j: (0, 0, 0, 0, j))
    up_tile = pl.BlockSpec((feats, BLK), lambda j: (0, j))
    down_tile = pl.BlockSpec((BLK, feats), lambda j: (j, 0))
    return pl.pallas_call(
        forward_kernel,
        grid=(hid // BLK,),
        in_specs=[scalars(), scalars(), *(whole(p.shape) for p in (own, near, rest)), up_tile, up_tile, down_tile],
        out_specs=[out, out],
        out_shape=[shape, shape],
        scratch_shapes=[pltpu.VMEM((tok, 2 * feats), BF16)],
        compiler_params=pltpu.CompilerParams(vmem_limit_bytes=28 << 20),
        cost_estimate=pl.CostEstimate(flops=6 * tok * feats * hid, bytes_accessed=14 << 20, transcendentals=0),
    )(core, mask, own, near, rest, w_gate, w_up, w_down)


def outputs_kernel(core, mask, two, rest, two_swapped, rest_swapped, wg, wu, wd, kept, sent, acts):
    i = pl.program_id(0)

    @pl.when(i == 0)
    def _():
        for side in range(3):
            acts[side] = acts_rows(side, two, rest, two_swapped, rest_swapped)

    width = wd.shape[1] // BLK
    blocks = wd.shape[0] // BLK

    def flag(k, j):
        return mask[i * width + k, j]

    down = jnp.concatenate(
        [
            jnp.concatenate(
                [keep(flag(k, j), wd[j * BLK : (j + 1) * BLK, k * BLK : (k + 1) * BLK]) for j in range(blocks)], axis=0
            )
            for k in range(width)
        ],
        axis=1,
    )
    output = jnp.dot(acts[0], down, preferred_element_type=F32)
    grad = None
    for side, w in ((1, wg), (2, wu)):
        weight = jnp.concatenate(
            [
                jnp.concatenate(
                    [keep(flag(k, j), w[k * BLK : (k + 1) * BLK, j * BLK : (j + 1) * BLK]) for j in range(blocks)],
                    axis=1,
                )
                for k in range(width)
            ],
            axis=0,
        )
        term = lax.dot_general(acts[side], weight, ROWS, preferred_element_type=F32)
        grad = term if grad is None else grad + term
    first = core[0] == 0
    for side, value in enumerate((output, grad)):
        value = value.reshape(4, -1, value.shape[1])
        kept[0, side] = value[0]
        kept[1, side] = jnp.where(first, value[2], value[1])
        sent[0, side] = jnp.where(first, value[1], value[2]).astype(BF16)
        sent[1, side] = value[3].astype(BF16)


def outputs(core, mask, acts, w_gate, w_up, w_down):
    hid, feats = w_down.shape
    tok = 32 * acts[0].shape[3]
    tile = min(256, feats)
    up_tile = pl.BlockSpec((tile, hid), lambda i: (i, 0))
    out = pl.BlockSpec((2, 2, tok // 4, tile), lambda i: (0, 0, 0, i))
    shape = (2, 2, tok // 4, feats)
    return pl.pallas_call(
        outputs_kernel,
        grid=(feats // tile,),
        in_specs=[
            scalars(),
            scalars(),
            *(whole(p.shape) for p in acts),
            up_tile,
            up_tile,
            pl.BlockSpec((hid, tile), lambda i: (0, i)),
        ],
        out_specs=[out, out],
        out_shape=[jax.ShapeDtypeStruct(shape, F32), jax.ShapeDtypeStruct(shape, BF16)],
        scratch_shapes=[pltpu.VMEM((3, tok, hid), BF16)],
        compiler_params=pltpu.CompilerParams(vmem_limit_bytes=28 << 20),
        cost_estimate=pl.CostEstimate(flops=6 * tok * hid * feats, bytes_accessed=12 << 20, transcendentals=0),
    )(core, mask, *acts, w_gate, w_up, w_down)


def weight_grads_kernel(core, mask, *refs):
    j = pl.program_id(0)
    mine, theirs, acts, their_acts = refs[:3], refs[3:6], refs[6:10], refs[10:14]
    grad_gate, grad_up, grad_down, tok_t, cot = refs[14:]
    feats = tok_t.shape[0]

    @pl.when(j == 0)
    def _():
        first = core[0] == 0
        rows = jnp.concatenate(row_pieces(first, *mine) + row_pieces(first, *theirs), axis=0)
        tok_t[...] = rows[:, :feats].T
        cot[...] = rows[:, feats:]

    hidden, gate, up = (
        jnp.concatenate([acts_rows(side, *acts), acts_rows(side, *their_acts)], axis=0) for side in range(3)
    )
    both = jnp.dot(tok_t[...], jnp.concatenate([gate, up], axis=1), preferred_element_type=F32).astype(BF16)
    down = lax.dot_general(hidden, cot[...], COLS, preferred_element_type=F32).astype(BF16)
    for k in range(feats // BLK):
        spot = pl.ds(k * BLK, BLK)
        grad_gate[spot, :] = keep(mask[k, j], both[k * BLK : (k + 1) * BLK, :BLK])
        grad_up[spot, :] = keep(mask[k, j], both[k * BLK : (k + 1) * BLK, BLK:])
        grad_down[:, spot] = keep(mask[k, j], down[:, k * BLK : (k + 1) * BLK])


def weight_grads(core, mask, mine, theirs, acts, their_acts):
    feats = mine[0].shape[1] // 2
    hid = acts[0].shape[-1]
    count = 8 * mine[0].shape[0]

    def act_tile(value):
        lead = value.shape[:-1]
        return pl.BlockSpec((*lead, BLK), lambda j: (0,) * len(lead) + (j,))

    up_tile = pl.BlockSpec((feats, BLK), lambda j: (0, j))
    return pl.pallas_call(
        weight_grads_kernel,
        grid=(hid // BLK,),
        in_specs=[
            scalars(),
            scalars(),
            *(whole(p.shape) for p in (*mine, *theirs)),
            *(act_tile(p) for p in (*acts, *their_acts)),
        ],
        out_specs=[up_tile, up_tile, pl.BlockSpec((BLK, feats), lambda j: (j, 0))],
        out_shape=[
            jax.ShapeDtypeStruct((feats, hid), BF16),
            jax.ShapeDtypeStruct((feats, hid), BF16),
            jax.ShapeDtypeStruct((hid, feats), BF16),
        ],
        scratch_shapes=[pltpu.VMEM((feats, count), BF16), pltpu.VMEM((count, feats), BF16)],
        compiler_params=pltpu.CompilerParams(vmem_limit_bytes=28 << 20),
        cost_estimate=pl.CostEstimate(flops=6 * count * hid * feats, bytes_accessed=20 << 20, transcendentals=0),
    )(core, mask, *mine, *theirs, *acts, *their_acts)


def frame(rows):
    quad = rows // 8
    x, z, core = lax.axis_index("x"), lax.axis_index("zh"), lax.axis_index("core")
    steps = jnp.array([[0, 1, 3, 2], [0, 3, 1, 2]], jnp.int32)
    spot = jnp.arange(4 * rows, dtype=jnp.int32)
    k, j, at_z, q = spot // rows, spot // (4 * quad) % 2, spot // quad % 4, spot % quad
    owner = core ^ j
    at_x = x ^ jnp.where(owner == 0, steps[0][k], steps[1][k])
    away = at_z ^ z
    piece = jnp.where(away == 0, 0, jnp.where(away == 2, 3, jnp.where((away == 1) == (core == 0), 1, 2)))
    wanted = piece * rows + (at_x * 2 + owner) * quad + q
    return (wanted[:, None] == spot[None, :]).astype(F32)


def local(inputs, out_grad, w_gate, w_up, w_down, block_mask):
    rows, feats = inputs.shape
    core = lax.axis_index("core").astype(jnp.int32).reshape(1)
    pick = frame(rows)

    own = jnp.concatenate([inputs, out_grad], axis=1)
    two = jnp.concatenate([own, exchange(own, "zh", 0)], axis=0)
    z_rows = jnp.concatenate([two, exchange(two, "zh", 1)], axis=0)
    z_rows = jnp.dot(pick.astype(BF16), z_rows, preferred_element_type=F32).astype(BF16)

    near = exchange(z_rows, "y", 0)
    rest = exchange(jnp.concatenate([z_rows, near], axis=0), "y", 1)
    other_z = swap(z_rows, "dp")
    mine = (z_rows, near, after(rest, other_z))

    kept, sent = forward(core, block_mask, *mine, w_gate, w_up, w_down)
    other_near = exchange(other_z, "y", 0)
    both = kept + swap(sent, "core")
    got = exchange(jnp.stack([both[1], both[3]]).astype(BF16), "x", 0).astype(F32)
    second = after((both[2] + got[1]).astype(BF16), other_near)
    gate_pre, up_pre, hidden_grad = both[0] + got[0] + exchange(second, "x", 1).astype(F32)
    sig = jax.nn.sigmoid(gate_pre)
    hidden = (gate_pre * sig * up_pre).astype(BF16)
    gate_grad = (hidden_grad * up_pre * sig * (1.0 + gate_pre * (1.0 - sig))).astype(BF16)
    up_grad = (hidden_grad * gate_pre * sig).astype(BF16)
    own_acts = jnp.stack([hidden, gate_grad, up_grad])

    def gather_x(value, *earlier):
        pair = after(jnp.stack([value, exchange(value, "x", 0)]), *earlier)
        return pair, exchange(pair, "x", 1)

    other_rest = exchange(jnp.concatenate([other_z, other_near], axis=0), "y", 1)
    theirs = (other_z, other_near, other_rest)
    pair, far = gather_x(own_acts)
    acts = (pair, far, swap(pair, "core"), swap(far, "core"))
    their_acts = swap(own_acts, "dp")

    kept, sent = outputs(core, block_mask, (*acts[:3], after(acts[3], other_rest, their_acts)), w_gate, w_up, w_down)
    their_pair, their_far = gather_x(after(their_acts, kept))
    both = kept + exchange(sent, "y", 0).astype(F32)
    second = after(both[1].astype(BF16), their_pair)
    total = both[0] + exchange(second, "y", 1).astype(F32)

    their_acts = (their_pair, their_far, swap(their_pair, "core"), swap(their_far, "core"))
    total = jnp.concatenate(
        [lax.dot_general(pick, side, COLS, precision="highest", preferred_element_type=F32) for side in total], axis=1
    ).reshape(4, rows, 2 * feats)
    got = exchange(jnp.stack([total[1], total[3]]).astype(BF16), "zh", 0).astype(F32)
    second = after((total[2] + got[1]).astype(BF16), their_far)
    total = (total[0] + got[0] + exchange(second, "zh", 1).astype(F32)).astype(BF16)

    grads = weight_grads(core, block_mask, mine, theirs, acts, their_acts)
    return total[:, :feats], total[:, feats:], *grads


def solution(mesh):
    split = Mesh(mesh.devices.reshape(2, 4, 4, 4, 2), ("dp", "y", "zh", "x", "core"))
    token_rows = P(("dp", "y", "zh"), ("x", "core"))
    weight_in = P(("x", "core"), ("y", "zh"))
    weight_out = P(("y", "zh"), ("x", "core"))
    return jax.shard_map(
        local,
        mesh=split,
        in_specs=(token_rows, token_rows, weight_in, weight_in, weight_out, weight_in),
        out_specs=(token_rows, token_rows, weight_in, weight_in, weight_out),
        check_vma=False,
    )
```

```python
import jax
import jax.numpy as jnp
from jax import lax
from jax.experimental import pallas as pl
from jax.experimental.pallas import tpu as pltpu
from jax.sharding import Mesh, PartitionSpec as P

BLK = 128
F32 = jnp.float32
BF16 = jnp.bfloat16

ROWS = (((1,), (1,)), ((), ()))
COLS = (((0,), (0,)), ((), ()))

PARTNERS = ((1, 3), (3, 1))


def exchange(value, axis, step):
    pairs = [(2 * i + c, 2 * (i ^ PARTNERS[c][step]) + c) for i in range(4) for c in range(2)]
    return lax.ppermute(value, (axis, "core"), pairs)


def swap(value, axis):
    return lax.ppermute(value, axis, [(0, 1), (1, 0)])


def after(value, *earlier):
    return lax.optimization_barrier((value, *earlier))[0]


def scalars():
    return pl.BlockSpec(memory_space=pltpu.SMEM)


def keep(flag, block):
    return jnp.where(flag > 0, block, jnp.zeros_like(block))


def row_pieces(first, own, near, rest):
    size = own.shape[0]
    other = rest[:size, :]
    return [own[...], jnp.where(first, near[...], other), jnp.where(first, other, near[...]), rest[size:, :]]


def acts_rows(side, two, rest, two_swapped, rest_swapped):
    pieces = [(two, two_swapped, 0), (two, two_swapped, 1), (rest, rest_swapped, 0), (rest, rest_swapped, 1)]
    return jnp.concatenate(
        [ref[k, side, y] for y in range(4) for mine, sibling, k in pieces for ref in (mine, sibling)], axis=0
    )


def call(kernel, outs, operands, flops, scratch=(), **grid):
    vmem = pl.BlockSpec(memory_space=pltpu.VMEM)
    return pl.pallas_call(
        kernel,
        in_specs=[scalars(), scalars(), *(vmem for _ in operands[2:])],
        out_specs=grid.pop("out_specs", [vmem] * len(outs)),
        out_shape=outs,
        scratch_shapes=list(scratch),
        compiler_params=pltpu.CompilerParams(vmem_limit_bytes=30 << 20),
        cost_estimate=pl.CostEstimate(flops=flops, bytes_accessed=1 << 20, transcendentals=0),
        **grid,
    )(*operands)


def blocks(count):
    return [slice(k * BLK, (k + 1) * BLK) for k in range(count)]


def masked(weight, rows, cols, flag):
    return jnp.concatenate(
        [
            jnp.concatenate(
                [keep(flag(r, c), weight[r * BLK : (r + 1) * BLK, c * BLK : (c + 1) * BLK]) for r in rows], axis=0
            )
            for c in cols
        ],
        axis=1,
    )


def split_rows(acc, side, cols, kept, sent):
    acc = acc.reshape(4, 4, 2, acc.shape[0] // 32, acc.shape[1])
    for k in range(4):
        kept[k, side, :, :, cols] = acc[:, k, 0]
        sent[k, side, :, :, cols] = acc[:, k, 1]


def gate_up_kernel(core, mask, own, near, rest, wg, wu, kept, sent):
    rows = jnp.concatenate(row_pieces(core[0] == 0, own, near, rest), axis=0)
    feat_blocks = range(wg.shape[0] // BLK)
    for j, cols in enumerate(blocks(wg.shape[1] // BLK)):
        weight = jnp.concatenate([masked(w, feat_blocks, [j], lambda r, c: mask[r, c]) for w in (wg, wu)], axis=1)
        pre = jnp.dot(rows, weight, preferred_element_type=F32)
        split_rows(pre[:, :BLK], 0, cols, kept, sent)
        split_rows(pre[:, BLK:], 1, cols, kept, sent)


def back_kernel(core, mask, own, near, rest, wd, kept, sent):
    rows = jnp.concatenate(row_pieces(core[0] == 0, own, near, rest), axis=0)
    hid_blocks, feat_blocks = wd.shape[0] // BLK, range(wd.shape[1] // BLK)
    for j in range(0, hid_blocks, 2):
        stop = min(j + 2, hid_blocks)
        weight = masked(wd, range(j, stop), feat_blocks, lambda r, c: mask[c, r])
        acc = lax.dot_general(rows, weight, ROWS, preferred_element_type=F32)
        split_rows(acc, 0, slice(j * BLK, stop * BLK), kept, sent)


def partial_sums(kernel, core, mask, pieces, weights, hid):
    tok, feats = 4 * pieces[0].shape[0], pieces[0].shape[1]
    sides = len(weights)
    shape = jax.ShapeDtypeStruct((4, sides, 4, tok // 32, hid), F32)
    return call(kernel, [shape, shape], (core, mask, *pieces, *weights), 2 * sides * tok * feats * hid)


def outputs_kernel(core, mask, two, rest, two_swapped, rest_swapped, wg, wu, wd, kept, sent):
    hidden, gate, up = (acts_rows(side, two, rest, two_swapped, rest_swapped) for side in range(3))
    first = core[0] == 0
    feat_blocks, hid_blocks = wg.shape[0] // BLK, range(wg.shape[1] // BLK)
    for i in range(0, feat_blocks, 2):
        span = range(i, min(i + 2, feat_blocks))
        cols = slice(i * BLK, span.stop * BLK)
        down = masked(wd, hid_blocks, span, lambda r, c: mask[c, r])
        output = jnp.dot(hidden, down, preferred_element_type=F32)
        grad = sum(
            lax.dot_general(
                value, masked(w, span, hid_blocks, lambda r, c: mask[r, c]), ROWS, preferred_element_type=F32
            )
            for value, w in ((gate, wg), (up, wu))
        )
        for side, value in enumerate((output, grad)):
            value = value.reshape(4, -1, value.shape[1])
            kept[0, side, :, cols] = value[0]
            kept[1, side, :, cols] = jnp.where(first, value[2], value[1])
            sent[0, side, :, cols] = jnp.where(first, value[1], value[2]).astype(BF16)
            sent[1, side, :, cols] = value[3].astype(BF16)


def outputs(core, mask, acts, w_gate, w_up, w_down):
    hid, feats = w_down.shape
    tok = 32 * acts[0].shape[3]
    shape = (2, 2, tok // 4, feats)
    outs = [jax.ShapeDtypeStruct(shape, F32), jax.ShapeDtypeStruct(shape, BF16)]
    return call(outputs_kernel, outs, (core, mask, *acts, w_gate, w_up, w_down), 6 * tok * hid * feats)


def own_grads_kernel(core, mask, *refs):
    tokens, cots, acts, both, down = refs[:3], refs[3:6], refs[6:10], refs[10], refs[11]
    first = core[0] == 0
    tok_t = jnp.concatenate(row_pieces(first, *tokens), axis=0).T
    cot = jnp.concatenate(row_pieces(first, *cots), axis=0)
    for j, cols in enumerate(blocks(acts[0].shape[-1] // BLK)):
        hidden, gate, up = (acts_rows(side, *(ref.at[:, :, :, :, cols] for ref in acts)) for side in range(3))
        both[j] = jnp.dot(tok_t, jnp.concatenate([gate, up], axis=1), preferred_element_type=F32)
        down[cols, :] = lax.dot_general(hidden, cot, COLS, preferred_element_type=F32)


def own_grads(core, mask, tokens, cots, acts):
    feats, hid, count = tokens[0].shape[1], acts[0].shape[-1], 4 * tokens[0].shape[0]
    outs = [
        jax.ShapeDtypeStruct((hid // BLK, feats, 2 * BLK), F32),
        jax.ShapeDtypeStruct((hid, feats), F32),
    ]
    return call(own_grads_kernel, outs, (core, mask, *tokens, *cots, *acts), 6 * count * feats * hid)


def all_grads_kernel(core, mask, *refs):
    theirs, acts, own_both, own_down = refs[:3], refs[3:7], refs[7], refs[8]
    grad_gate, grad_up, grad_down, tok_t, cot = refs[9:]
    j = pl.program_id(0)
    feats = tok_t.shape[0]

    @pl.when(j == 0)
    def _():
        rows = jnp.concatenate(row_pieces(core[0] == 0, *theirs), axis=0)
        tok_t[...] = rows[:, :feats].T
        cot[...] = rows[:, feats:]

    cols = pl.ds(pl.multiple_of(j * BLK, BLK), BLK)
    hidden, gate, up = (acts_rows(side, *(ref.at[:, :, :, :, cols] for ref in acts)) for side in range(3))
    both = jnp.dot(tok_t[...], jnp.concatenate([gate, up], axis=1), preferred_element_type=F32)
    both = (both + own_both[j]).astype(BF16)
    down = lax.dot_general(hidden, cot[...], COLS, preferred_element_type=F32)
    down = (down + own_down[cols, :]).astype(BF16)
    for k, spot in enumerate(blocks(feats // BLK)):
        grad_gate[spot, :] = keep(mask[k, j], both[spot, :BLK])
        grad_up[spot, :] = keep(mask[k, j], both[spot, BLK:])
        grad_down[:, spot] = keep(mask[k, j], down[:, spot])


def all_grads(core, mask, theirs, acts, own):
    feats, hid, count = theirs[0].shape[1] // 2, acts[0].shape[-1], 4 * theirs[0].shape[0]
    up = jax.ShapeDtypeStruct((feats, hid), BF16)
    up_tile = pl.BlockSpec((feats, BLK), lambda j: (0, j))
    return call(
        all_grads_kernel,
        [up, up, jax.ShapeDtypeStruct((hid, feats), BF16)],
        (core, mask, *theirs, *acts, *own),
        6 * count * feats * hid,
        [pltpu.VMEM((feats, count), BF16), pltpu.VMEM((count, feats), BF16)],
        grid=(hid // BLK,),
        out_specs=[up_tile, up_tile, pl.BlockSpec((BLK, feats), lambda j: (j, 0))],
    )


def frame(rows):
    quad = rows // 8
    x, z, core = lax.axis_index("x"), lax.axis_index("zh"), lax.axis_index("core")
    steps = jnp.array([[0, 1, 3, 2], [0, 3, 1, 2]], jnp.int32)
    spot = jnp.arange(4 * rows, dtype=jnp.int32)
    k, j, at_z, q = spot // rows, spot // (4 * quad) % 2, spot // quad % 4, spot % quad
    owner = core ^ j
    at_x = x ^ jnp.where(owner == 0, steps[0][k], steps[1][k])
    away = at_z ^ z
    piece = jnp.where(away == 0, 0, jnp.where(away == 2, 3, jnp.where((away == 1) == (core == 0), 1, 2)))
    wanted = piece * rows + (at_x * 2 + owner) * quad + q
    return (wanted[:, None] == spot[None, :]).astype(F32)


def gather(own, axis, wrap=jnp.concatenate):
    two = wrap([own, exchange(own, axis, 0)])
    return two, exchange(two, axis, 1)


def scatter(kept, sent, axis, *earlier):
    both = kept + exchange(sent, axis, 0).astype(F32)
    return both[0] + exchange(after(both[1].astype(BF16), *earlier), axis, 1).astype(F32)


def local(inputs, out_grad, w_gate, w_up, w_down, block_mask):
    rows, feats = inputs.shape
    hid = w_gate.shape[1]
    core = lax.axis_index("core").astype(jnp.int32).reshape(1)
    pick = frame(rows)

    def pick_rows(two, rest):
        z_rows = jnp.concatenate([two, rest], axis=0)
        return jnp.dot(pick.astype(BF16), z_rows, preferred_element_type=F32).astype(BF16)

    tok, cot = inputs, out_grad
    tok_near, cot_near = exchange(tok, "zh", 0), exchange(cot, "zh", 0)
    tok = after(jnp.concatenate([tok, tok_near], axis=0), cot_near)
    cot = jnp.concatenate([cot, cot_near], axis=0)
    tok, cot = pick_rows(tok, exchange(tok, "zh", 1)), pick_rows(cot, exchange(cot, "zh", 1))
    tok_near, cot_near = exchange(tok, "y", 0), exchange(cot, "y", 0)
    tok_rest = exchange(after(jnp.concatenate([tok, tok_near], axis=0), cot), "y", 1)
    cot_rest = exchange(jnp.concatenate([cot, cot_near], axis=0), "y", 1)
    tokens, cots = (tok, tok_near, tok_rest), (cot, cot_near, cot_rest)
    their_z = swap(jnp.concatenate([tok, cot], axis=1), "dp")

    pieces = (tok, tok_near, after(tok_rest, cot_near))
    pre_kept, pre_sent = partial_sums(gate_up_kernel, core, block_mask, pieces, (w_gate, w_up), hid)
    pre_got = swap(pre_sent, "core")
    pieces = (cot, cot_near, after(cot_rest, their_z))
    back_kept, back_sent = partial_sums(back_kernel, core, block_mask, pieces, (w_down,), hid)
    their_near = exchange(their_z, "y", 0)

    pre = pre_kept + pre_got
    back = back_kept + swap(back_sent, "core")
    kept = jnp.stack([jnp.concatenate([pre[k], back[k]]) for k in (0, 2)])
    sent = jnp.stack([jnp.concatenate([pre[k].astype(BF16), back[k].astype(BF16)]) for k in (1, 3)])
    gate_pre, up_pre, hidden_grad = scatter(kept, sent, "x", their_near)
    sig = jax.nn.sigmoid(gate_pre)
    hidden = (gate_pre * sig * up_pre).astype(BF16)
    gate_grad = (hidden_grad * up_pre * sig * (1.0 + gate_pre * (1.0 - sig))).astype(BF16)
    up_grad = (hidden_grad * gate_pre * sig).astype(BF16)
    own_acts = jnp.stack([hidden, gate_grad, up_grad])

    pair, far = gather(own_acts, "x", jnp.stack)
    their_acts = swap(own_acts, "dp")
    far = after(far, their_acts)
    acts = (pair, far, swap(pair, "core"), swap(far, "core"))
    their_rest = exchange(jnp.concatenate([their_z, their_near], axis=0), "y", 1)

    kept, sent = outputs(core, block_mask, acts, w_gate, w_up, w_down)
    their_pair = jnp.stack([their_acts, exchange(after(their_acts, far), "x", 0)])
    own = own_grads(core, block_mask, tokens, cots, acts)
    their_far = exchange(their_pair, "x", 1)
    both = kept + after(exchange(after(sent, their_rest), "y", 0)).astype(F32)
    second = exchange(after(both[1].astype(BF16), their_pair), "y", 1)
    total = both[0] + second.astype(F32)

    total = after(total, their_far)
    total = jnp.concatenate(
        [lax.dot_general(pick, side, COLS, precision="highest", preferred_element_type=F32) for side in total], axis=1
    ).reshape(4, rows, 2 * feats)
    kept, sent = jnp.stack([total[0], total[2]]), jnp.stack([total[1], total[3]]).astype(BF16)
    theirs = (their_z, their_near, their_rest)
    their_acts = (their_pair, their_far, swap(their_pair, "core"), swap(their_far, "core"))
    grads = all_grads(core, block_mask, theirs, their_acts, own)
    total = scatter(kept, sent, "zh", grads[0]).astype(BF16)
    return total[:, :feats], total[:, feats:], *grads


def solution(mesh):
    split = Mesh(mesh.devices.reshape(2, 4, 4, 4, 2), ("dp", "y", "zh", "x", "core"))
    token_rows = P(("dp", "y", "zh"), ("x", "core"))
    weight_in = P(("x", "core"), ("y", "zh"))
    weight_out = P(("y", "zh"), ("x", "core"))
    return jax.shard_map(
        local,
        mesh=split,
        in_specs=(token_rows, token_rows, weight_in, weight_in, weight_out, weight_in),
        out_specs=(token_rows, token_rows, weight_in, weight_in, weight_out),
        check_vma=False,
    )
```

```python
import jax
import jax.numpy as jnp
from jax import lax
from jax.experimental import pallas as pl
from jax.experimental.pallas import tpu as pltpu
from jax.sharding import Mesh, PartitionSpec as P

BLK = 128
F32 = jnp.float32
BF16 = jnp.bfloat16

ROWS = (((1,), (1,)), ((), ()))
COLS = (((0,), (0,)), ((), ()))

PARTNERS = ((1, 3), (3, 1))


def exchange(value, axis, step):
    pairs = [(2 * i + c, 2 * (i ^ PARTNERS[c][step]) + c) for i in range(4) for c in range(2)]
    return lax.ppermute(value, (axis, "core"), pairs)


def swap(value, axis):
    return lax.ppermute(value, axis, [(0, 1), (1, 0)])


def after(value, *earlier):
    return lax.optimization_barrier((value, *earlier))[0]


def scalars():
    return pl.BlockSpec(memory_space=pltpu.SMEM)


def keep(flag, block):
    return jnp.where(flag > 0, block, jnp.zeros_like(block))


def row_pieces(first, own, near, rest):
    size = own.shape[0]
    other = rest[:size, :]
    return [own[...], jnp.where(first, near[...], other), jnp.where(first, other, near[...]), rest[size:, :]]


def acts_rows(side, two, rest, two_swapped, rest_swapped):
    pieces = [(two, two_swapped, 0), (two, two_swapped, 1), (rest, rest_swapped, 0), (rest, rest_swapped, 1)]
    return jnp.concatenate(
        [ref[k, side, y] for y in range(4) for mine, sibling, k in pieces for ref in (mine, sibling)], axis=0
    )


def call(kernel, outs, operands):
    vmem = pl.BlockSpec(memory_space=pltpu.VMEM)
    return pl.pallas_call(
        kernel,
        in_specs=[scalars(), scalars(), *(vmem for _ in operands[2:])],
        out_specs=[vmem] * len(outs),
        out_shape=outs,
        compiler_params=pltpu.CompilerParams(vmem_limit_bytes=30 << 20),
        cost_estimate=pl.CostEstimate(flops=1 << 20, bytes_accessed=1 << 10, transcendentals=0),
    )(*operands)


def blocks(count):
    return [slice(k * BLK, (k + 1) * BLK) for k in range(count)]


def masked(weight, rows, cols, flag):
    return jnp.concatenate(
        [
            jnp.concatenate(
                [keep(flag(r, c), weight[r * BLK : (r + 1) * BLK, c * BLK : (c + 1) * BLK]) for r in rows], axis=0
            )
            for c in cols
        ],
        axis=1,
    )


def split_rows(acc, side, cols, kept, sent):
    acc = acc.reshape(4, 4, 2, acc.shape[0] // 32, acc.shape[1])
    for k in range(4):
        kept[k, side, :, :, cols] = acc[:, k, 0]
        sent[k, side, :, :, cols] = acc[:, k, 1]


def gate_up_kernel(core, mask, own, near, rest, wg, wu, kept, sent):
    rows = jnp.concatenate(row_pieces(core[0] == 0, own, near, rest), axis=0)
    feat_blocks = range(wg.shape[0] // BLK)
    for j, cols in enumerate(blocks(wg.shape[1] // BLK)):
        weight = jnp.concatenate([masked(w, feat_blocks, [j], lambda r, c: mask[r, c]) for w in (wg, wu)], axis=1)
        pre = jnp.dot(rows, weight, preferred_element_type=F32)
        split_rows(pre[:, :BLK], 0, cols, kept, sent)
        split_rows(pre[:, BLK:], 1, cols, kept, sent)


def back_kernel(core, mask, own, near, rest, wd, kept, sent):
    rows = jnp.concatenate(row_pieces(core[0] == 0, own, near, rest), axis=0)
    hid_blocks, feat_blocks = wd.shape[0] // BLK, range(wd.shape[1] // BLK)
    for j in range(0, hid_blocks, 2):
        stop = min(j + 2, hid_blocks)
        weight = masked(wd, range(j, stop), feat_blocks, lambda r, c: mask[c, r])
        acc = lax.dot_general(rows, weight, ROWS, preferred_element_type=F32)
        split_rows(acc, 0, slice(j * BLK, stop * BLK), kept, sent)


def partial_sums(kernel, core, mask, pieces, weights, hid):
    tok, feats = 4 * pieces[0].shape[0], pieces[0].shape[1]
    sides = len(weights)
    shape = jax.ShapeDtypeStruct((4, sides, 4, tok // 32, hid), F32)
    return call(kernel, [shape, shape], (core, mask, *pieces, *weights))


def outputs_kernel(core, mask, two, rest, two_swapped, rest_swapped, wg, wu, wd, kept, sent):
    hidden, gate, up = (acts_rows(side, two, rest, two_swapped, rest_swapped) for side in range(3))
    first = core[0] == 0
    feat_blocks, hid_blocks = wg.shape[0] // BLK, range(wg.shape[1] // BLK)
    for i in range(0, feat_blocks, 2):
        span = range(i, min(i + 2, feat_blocks))
        cols = slice(i * BLK, span.stop * BLK)
        down = masked(wd, hid_blocks, span, lambda r, c: mask[c, r])
        output = jnp.dot(hidden, down, preferred_element_type=F32)
        grad = sum(
            lax.dot_general(
                value, masked(w, span, hid_blocks, lambda r, c: mask[r, c]), ROWS, preferred_element_type=F32
            )
            for value, w in ((gate, wg), (up, wu))
        )
        for side, value in enumerate((output, grad)):
            value = value.reshape(4, -1, value.shape[1])
            kept[0, side, :, cols] = value[0]
            kept[1, side, :, cols] = jnp.where(first, value[2], value[1])
            sent[0, side, :, cols] = jnp.where(first, value[1], value[2]).astype(BF16)
            sent[1, side, :, cols] = value[3].astype(BF16)


def outputs(core, mask, acts, w_gate, w_up, w_down):
    hid, feats = w_down.shape
    tok = 32 * acts[0].shape[3]
    shape = (2, 2, tok // 4, feats)
    outs = [jax.ShapeDtypeStruct(shape, F32), jax.ShapeDtypeStruct(shape, BF16)]
    return call(outputs_kernel, outs, (core, mask, *acts, w_gate, w_up, w_down))


def own_grads_kernel(core, mask, *refs):
    tokens, cots, acts, both, down = refs[:3], refs[3:6], refs[6:10], refs[10], refs[11]
    first = core[0] == 0
    tok_t = jnp.concatenate(row_pieces(first, *tokens), axis=0).T
    cot = jnp.concatenate(row_pieces(first, *cots), axis=0)
    for j, cols in enumerate(blocks(acts[0].shape[-1] // BLK)):
        hidden, gate, up = (acts_rows(side, *(ref.at[:, :, :, :, cols] for ref in acts)) for side in range(3))
        both[j] = jnp.dot(tok_t, jnp.concatenate([gate, up], axis=1), preferred_element_type=F32)
        down[cols, :] = lax.dot_general(hidden, cot, COLS, preferred_element_type=F32)


def own_grads(core, mask, tokens, cots, acts):
    feats, hid = tokens[0].shape[1], acts[0].shape[-1]
    outs = [
        jax.ShapeDtypeStruct((hid // BLK, feats, 2 * BLK), F32),
        jax.ShapeDtypeStruct((hid, feats), F32),
    ]
    return call(own_grads_kernel, outs, (core, mask, *tokens, *cots, *acts))


def all_grads_kernel(core, mask, *refs):
    theirs, acts, own_both, own_down = refs[:3], refs[3:7], refs[7], refs[8]
    grad_gate, grad_up, grad_down = refs[9:]
    feats = own_down.shape[1]
    rows = jnp.concatenate(row_pieces(core[0] == 0, *theirs), axis=0)
    tok_t, cot = rows[:, :feats].T, rows[:, feats:]
    for j, cols in enumerate(blocks(acts[0].shape[-1] // BLK)):
        hidden, gate, up = (acts_rows(side, *(ref.at[:, :, :, :, cols] for ref in acts)) for side in range(3))
        both = jnp.dot(tok_t, jnp.concatenate([gate, up], axis=1), preferred_element_type=F32)
        both = (both + own_both[j]).astype(BF16)
        down = lax.dot_general(hidden, cot, COLS, preferred_element_type=F32)
        down = (down + own_down[cols, :]).astype(BF16)
        for k, spot in enumerate(blocks(feats // BLK)):
            grad_gate[spot, cols] = keep(mask[k, j], both[spot, :BLK])
            grad_up[spot, cols] = keep(mask[k, j], both[spot, BLK:])
            grad_down[cols, spot] = keep(mask[k, j], down[:, spot])


def all_grads(core, mask, theirs, acts, own):
    feats, hid = theirs[0].shape[1] // 2, acts[0].shape[-1]
    up = jax.ShapeDtypeStruct((feats, hid), BF16)
    outs = [up, up, jax.ShapeDtypeStruct((hid, feats), BF16)]
    return call(all_grads_kernel, outs, (core, mask, *theirs, *acts, *own))


def frame(rows):
    quad = rows // 8
    x, z, core = lax.axis_index("x"), lax.axis_index("zh"), lax.axis_index("core")
    steps = jnp.array([[0, 1, 3, 2], [0, 3, 1, 2]], jnp.int32)
    spot = jnp.arange(4 * rows, dtype=jnp.int32)
    k, j, at_z, q = spot // rows, spot // (4 * quad) % 2, spot // quad % 4, spot % quad
    owner = core ^ j
    at_x = x ^ jnp.where(owner == 0, steps[0][k], steps[1][k])
    away = at_z ^ z
    piece = jnp.where(away == 0, 0, jnp.where(away == 2, 3, jnp.where((away == 1) == (core == 0), 1, 2)))
    wanted = piece * rows + (at_x * 2 + owner) * quad + q
    return (wanted[:, None] == spot[None, :]).astype(F32)


def gather(own, axis, wrap=jnp.concatenate):
    two = wrap([own, exchange(own, axis, 0)])
    return two, exchange(two, axis, 1)


def scatter(kept, sent, axis, *earlier):
    both = kept + exchange(sent, axis, 0).astype(F32)
    return both[0] + exchange(after(both[1].astype(BF16), *earlier), axis, 1).astype(F32)


def local(inputs, out_grad, w_gate, w_up, w_down, block_mask):
    rows, feats = inputs.shape
    hid = w_gate.shape[1]
    core = lax.axis_index("core").astype(jnp.int32).reshape(1)
    pick = frame(rows)

    def pick_rows(two, rest):
        z_rows = jnp.concatenate([two, rest], axis=0)
        return jnp.dot(pick.astype(BF16), z_rows, preferred_element_type=F32).astype(BF16)

    tok, cot = inputs, out_grad
    tok_near, cot_near = exchange(tok, "zh", 0), exchange(cot, "zh", 0)
    tok = after(jnp.concatenate([tok, tok_near], axis=0), cot_near)
    cot = jnp.concatenate([cot, cot_near], axis=0)
    tok, cot = pick_rows(tok, exchange(tok, "zh", 1)), pick_rows(cot, exchange(cot, "zh", 1))
    tok_near, cot_near = exchange(tok, "y", 0), exchange(cot, "y", 0)
    tok_rest = exchange(after(jnp.concatenate([tok, tok_near], axis=0), cot), "y", 1)
    cot_rest = exchange(jnp.concatenate([cot, cot_near], axis=0), "y", 1)
    tokens, cots = (tok, tok_near, tok_rest), (cot, cot_near, cot_rest)
    their_z = swap(jnp.concatenate([tok, cot], axis=1), "dp")

    pieces = (tok, tok_near, after(tok_rest, cot_near))
    pre_kept, pre_sent = partial_sums(gate_up_kernel, core, block_mask, pieces, (w_gate, w_up), hid)
    pre_got = swap(pre_sent, "core")
    pieces = (cot, cot_near, after(cot_rest, their_z))
    back_kept, back_sent = partial_sums(back_kernel, core, block_mask, pieces, (w_down,), hid)
    their_near = exchange(their_z, "y", 0)

    pre = pre_kept + pre_got
    back = back_kept + swap(back_sent, "core")
    kept = jnp.stack([jnp.concatenate([pre[k], back[k]]) for k in (0, 2)])
    sent = jnp.stack([jnp.concatenate([pre[k].astype(BF16), back[k].astype(BF16)]) for k in (1, 3)])
    gate_pre, up_pre, hidden_grad = scatter(kept, sent, "x", their_near)
    sig = jax.nn.sigmoid(gate_pre)
    hidden = (gate_pre * sig * up_pre).astype(BF16)
    gate_grad = (hidden_grad * up_pre * sig * (1.0 + gate_pre * (1.0 - sig))).astype(BF16)
    up_grad = (hidden_grad * gate_pre * sig).astype(BF16)
    own_acts = jnp.stack([hidden, gate_grad, up_grad])

    pair, far = gather(own_acts, "x", jnp.stack)
    their_acts = swap(own_acts, "dp")
    far = after(far, their_acts)
    acts = (pair, far, swap(pair, "core"), swap(far, "core"))
    their_rest = exchange(jnp.concatenate([their_z, their_near], axis=0), "y", 1)

    kept, sent = outputs(core, block_mask, acts, w_gate, w_up, w_down)
    their_pair = jnp.stack([their_acts, exchange(after(their_acts, far), "x", 0)])
    own = own_grads(core, block_mask, tokens, cots, acts)
    their_far = exchange(their_pair, "x", 1)
    both = kept + exchange(after(sent, their_rest), "y", 0).astype(F32)
    second = exchange(after(both[1].astype(BF16), own[0], their_pair), "y", 1)
    total = both[0] + second.astype(F32)

    total = after(total, their_far)
    total = jnp.concatenate(
        [lax.dot_general(pick, side, COLS, precision="highest", preferred_element_type=F32) for side in total], axis=1
    ).reshape(4, rows, 2 * feats)
    kept, sent = jnp.stack([total[0], total[2]]), jnp.stack([total[1], total[3]]).astype(BF16)
    theirs = (their_z, their_near, their_rest)
    their_acts = (their_pair, their_far, swap(their_pair, "core"), swap(their_far, "core"))
    grads = all_grads(core, block_mask, theirs, their_acts, own)
    total = scatter(kept, sent, "zh", grads[0]).astype(BF16)
    return total[:, :feats], total[:, feats:], *grads


def solution(mesh):
    split = Mesh(mesh.devices.reshape(2, 4, 4, 4, 2), ("dp", "y", "zh", "x", "core"))
    token_rows = P(("dp", "y", "zh"), ("x", "core"))
    weight_in = P(("x", "core"), ("y", "zh"))
    weight_out = P(("y", "zh"), ("x", "core"))
    return jax.shard_map(
        local,
        mesh=split,
        in_specs=(token_rows, token_rows, weight_in, weight_in, weight_out, weight_in),
        out_specs=(token_rows, token_rows, weight_in, weight_in, weight_out),
        check_vma=False,
    )
```

```python
import jax
import jax.numpy as jnp
from jax import lax
from jax.experimental import pallas as pl
from jax.experimental.pallas import tpu as pltpu
from jax.sharding import Mesh, PartitionSpec as P

BLK = 128
F32 = jnp.float32
BF16 = jnp.bfloat16

ROWS = (((1,), (1,)), ((), ()))
COLS = (((0,), (0,)), ((), ()))

PARTNERS = ((1, 3), (3, 1))


def exchange(value, axis, step):
    pairs = [(2 * i + c, 2 * (i ^ PARTNERS[c][step]) + c) for i in range(4) for c in range(2)]
    return lax.ppermute(value, (axis, "core"), pairs)


def across(value, axis):
    pairs = [(2 * i + c, 2 * (i ^ 2) + c) for i in range(4) for c in range(2)]
    return lax.ppermute(value, (axis, "core"), pairs)


def swap(value, axis):
    return lax.ppermute(value, axis, [(0, 1), (1, 0)])


def after(value, *earlier):
    return lax.optimization_barrier((value, *earlier))[0]


def scalars():
    return pl.BlockSpec(memory_space=pltpu.SMEM)


def keep(flag, block):
    return jnp.where(flag > 0, block, jnp.zeros_like(block))


def row_pieces(first, own, near, rest):
    size = own.shape[0]
    other = rest[:size, :]
    return [own[...], jnp.where(first, near[...], other), jnp.where(first, other, near[...]), rest[size:, :]]


def acts_rows(side, two, rest, two_swapped, rest_swapped):
    pieces = [(two, two_swapped, 0), (two, two_swapped, 1), (rest, rest_swapped, 0), (rest, rest_swapped, 1)]
    return jnp.concatenate(
        [ref[k, side, y] for y in range(4) for mine, sibling, k in pieces for ref in (mine, sibling)], axis=0
    )


def call(kernel, outs, operands):
    vmem = pl.BlockSpec(memory_space=pltpu.VMEM)
    return pl.pallas_call(
        kernel,
        in_specs=[scalars(), scalars(), *(vmem for _ in operands[2:])],
        out_specs=[vmem] * len(outs),
        out_shape=outs,
        compiler_params=pltpu.CompilerParams(vmem_limit_bytes=30 << 20),
        cost_estimate=pl.CostEstimate(flops=1 << 20, bytes_accessed=1 << 10, transcendentals=0),
    )(*operands)


def blocks(count):
    return [slice(k * BLK, (k + 1) * BLK) for k in range(count)]


def masked(weight, rows, cols, flag):
    return jnp.concatenate(
        [
            jnp.concatenate(
                [keep(flag(r, c), weight[r * BLK : (r + 1) * BLK, c * BLK : (c + 1) * BLK]) for r in rows], axis=0
            )
            for c in cols
        ],
        axis=1,
    )


def split_rows(acc, side, cols, kept, sent):
    acc = acc.reshape(4, 4, 2, acc.shape[0] // 32, acc.shape[1])
    for k in range(4):
        kept[k, side, :, :, cols] = acc[:, k, 0]
        sent[k, side, :, :, cols] = acc[:, k, 1]


def gate_up_kernel(core, mask, own, near, rest, wg, wu, kept, sent):
    rows = jnp.concatenate(row_pieces(core[0] == 0, own, near, rest), axis=0)
    feat_blocks = range(wg.shape[0] // BLK)
    for j, cols in enumerate(blocks(wg.shape[1] // BLK)):
        weight = jnp.concatenate([masked(w, feat_blocks, [j], lambda r, c: mask[r, c]) for w in (wg, wu)], axis=1)
        pre = jnp.dot(rows, weight, preferred_element_type=F32)
        split_rows(pre[:, :BLK], 0, cols, kept, sent)
        split_rows(pre[:, BLK:], 1, cols, kept, sent)


def back_kernel(core, mask, own, near, rest, wd, kept, sent):
    rows = jnp.concatenate(row_pieces(core[0] == 0, own, near, rest), axis=0)
    hid_blocks, feat_blocks = wd.shape[0] // BLK, range(wd.shape[1] // BLK)
    for j in range(0, hid_blocks, 2):
        stop = min(j + 2, hid_blocks)
        weight = masked(wd, range(j, stop), feat_blocks, lambda r, c: mask[c, r])
        acc = lax.dot_general(rows, weight, ROWS, preferred_element_type=F32)
        split_rows(acc, 0, slice(j * BLK, stop * BLK), kept, sent)


def partial_sums(kernel, core, mask, pieces, weights, hid):
    tok, feats = 4 * pieces[0].shape[0], pieces[0].shape[1]
    sides = len(weights)
    shape = jax.ShapeDtypeStruct((4, sides, 4, tok // 32, hid), F32)
    return call(kernel, [shape, shape], (core, mask, *pieces, *weights))


def outputs_kernel(core, mask, two, rest, two_swapped, rest_swapped, wg, wu, wd, kept, sent):
    hidden, gate, up = (acts_rows(side, two, rest, two_swapped, rest_swapped) for side in range(3))
    first = core[0] == 0
    feat_blocks, hid_blocks = wg.shape[0] // BLK, range(wg.shape[1] // BLK)
    for i in range(0, feat_blocks, 2):
        span = range(i, min(i + 2, feat_blocks))
        cols = slice(i * BLK, span.stop * BLK)
        down = masked(wd, hid_blocks, span, lambda r, c: mask[c, r])
        output = jnp.dot(hidden, down, preferred_element_type=F32)
        grad = sum(
            lax.dot_general(
                value, masked(w, span, hid_blocks, lambda r, c: mask[r, c]), ROWS, preferred_element_type=F32
            )
            for value, w in ((gate, wg), (up, wu))
        )
        for side, value in enumerate((output, grad)):
            value = value.reshape(4, -1, value.shape[1])
            kept[0, side, :, cols] = value[0]
            kept[1, side, :, cols] = jnp.where(first, value[2], value[1])
            sent[0, side, :, cols] = jnp.where(first, value[1], value[2]).astype(BF16)
            sent[1, side, :, cols] = value[3].astype(BF16)


def outputs(core, mask, acts, w_gate, w_up, w_down):
    hid, feats = w_down.shape
    tok = 32 * acts[0].shape[3]
    shape = (2, 2, tok // 4, feats)
    outs = [jax.ShapeDtypeStruct(shape, F32), jax.ShapeDtypeStruct(shape, BF16)]
    return call(outputs_kernel, outs, (core, mask, *acts, w_gate, w_up, w_down))


def own_grads_kernel(core, mask, *refs):
    tokens, cots, acts, both, down = refs[:3], refs[3:6], refs[6:10], refs[10], refs[11]
    first = core[0] == 0
    tok_t = jnp.concatenate(row_pieces(first, *tokens), axis=0).T
    cot = jnp.concatenate(row_pieces(first, *cots), axis=0)
    for j, cols in enumerate(blocks(acts[0].shape[-1] // BLK)):
        hidden, gate, up = (acts_rows(side, *(ref.at[:, :, :, :, cols] for ref in acts)) for side in range(3))
        both[j] = jnp.dot(tok_t, jnp.concatenate([gate, up], axis=1), preferred_element_type=F32)
        down[cols, :] = lax.dot_general(hidden, cot, COLS, preferred_element_type=F32)


def own_grads(core, mask, tokens, cots, acts):
    feats, hid = tokens[0].shape[1], acts[0].shape[-1]
    outs = [
        jax.ShapeDtypeStruct((hid // BLK, feats, 2 * BLK), F32),
        jax.ShapeDtypeStruct((hid, feats), F32),
    ]
    return call(own_grads_kernel, outs, (core, mask, *tokens, *cots, *acts))


def all_grads_kernel(core, mask, *refs):
    theirs, acts, own_both, own_down = refs[:3], refs[3:7], refs[7], refs[8]
    grad_gate, grad_up, grad_down = refs[9:]
    feats = own_down.shape[1]
    rows = jnp.concatenate(row_pieces(core[0] == 0, *theirs), axis=0)
    tok_t, cot = rows[:, :feats].T, rows[:, feats:]
    for j, cols in enumerate(blocks(acts[0].shape[-1] // BLK)):
        hidden, gate, up = (acts_rows(side, *(ref.at[:, :, :, :, cols] for ref in acts)) for side in range(3))
        both = jnp.dot(tok_t, jnp.concatenate([gate, up], axis=1), preferred_element_type=F32)
        both = (both + own_both[j]).astype(BF16)
        down = lax.dot_general(hidden, cot, COLS, preferred_element_type=F32)
        down = (down + own_down[cols, :]).astype(BF16)
        for k, spot in enumerate(blocks(feats // BLK)):
            grad_gate[spot, cols] = keep(mask[k, j], both[spot, :BLK])
            grad_up[spot, cols] = keep(mask[k, j], both[spot, BLK:])
            grad_down[cols, spot] = keep(mask[k, j], down[:, spot])


def all_grads(core, mask, theirs, acts, own):
    feats, hid = theirs[0].shape[1] // 2, acts[0].shape[-1]
    up = jax.ShapeDtypeStruct((feats, hid), BF16)
    outs = [up, up, jax.ShapeDtypeStruct((hid, feats), BF16)]
    return call(all_grads_kernel, outs, (core, mask, *theirs, *acts, *own))


def frame(rows):
    quad = rows // 8
    x, z, core = lax.axis_index("x"), lax.axis_index("zh"), lax.axis_index("core")
    steps = jnp.array([[0, 1, 3, 2], [0, 3, 1, 2]], jnp.int32)
    spot = jnp.arange(4 * rows, dtype=jnp.int32)
    k, j, at_z, q = spot // rows, spot // (4 * quad) % 2, spot // quad % 4, spot % quad
    owner = core ^ j
    at_x = x ^ jnp.where(owner == 0, steps[0][k], steps[1][k])
    away = at_z ^ z
    piece = jnp.where(away == 0, 0, jnp.where(away == 2, 3, jnp.where((away == 1) == (core == 0), 1, 2)))
    wanted = piece * rows + (at_x * 2 + owner) * quad + q
    return (wanted[:, None] == spot[None, :]).astype(F32)


def gather(own, axis, wrap=jnp.concatenate):
    two = wrap([own, exchange(own, axis, 0)])
    return two, exchange(two, axis, 1)


def scatter(kept, sent, axis, *earlier):
    both = kept + exchange(sent, axis, 0).astype(F32)
    return both[0] + exchange(after(both[1].astype(BF16), *earlier), axis, 1).astype(F32)


def local(inputs, out_grad, w_gate, w_up, w_down, block_mask):
    rows, feats = inputs.shape
    hid = w_gate.shape[1]
    core = lax.axis_index("core").astype(jnp.int32).reshape(1)
    pick = frame(rows)

    def pick_rows(two, rest):
        z_rows = jnp.concatenate([two, rest], axis=0)
        return jnp.dot(pick.astype(BF16), z_rows, preferred_element_type=F32).astype(BF16)

    tok, cot = inputs, out_grad
    tok_near, cot_near = exchange(tok, "zh", 0), exchange(cot, "zh", 0)
    tok = after(jnp.concatenate([tok, tok_near], axis=0), cot_near)
    cot = jnp.concatenate([cot, cot_near], axis=0)
    tok, cot = pick_rows(tok, exchange(tok, "zh", 1)), pick_rows(cot, exchange(cot, "zh", 1))
    tok_near, cot_near = exchange(tok, "y", 0), exchange(cot, "y", 0)
    tok_rest = exchange(after(jnp.concatenate([tok, tok_near], axis=0), cot), "y", 1)
    cot_rest = exchange(jnp.concatenate([cot, cot_near], axis=0), "y", 1)
    tokens, cots = (tok, tok_near, tok_rest), (cot, cot_near, cot_rest)
    their_z = swap(jnp.concatenate([tok, cot], axis=1), "dp")

    pieces = (tok, tok_near, after(tok_rest, cot_near))
    pre_kept, pre_sent = partial_sums(gate_up_kernel, core, block_mask, pieces, (w_gate, w_up), hid)
    pre_got = swap(pre_sent, "core")
    pieces = (cot, cot_near, after(cot_rest, their_z))
    back_kept, back_sent = partial_sums(back_kernel, core, block_mask, pieces, (w_down,), hid)
    their_near = exchange(their_z, "y", 0)

    pre = pre_kept + pre_got
    back = back_kept + swap(back_sent, "core")
    kept = jnp.stack([jnp.concatenate([pre[k], back[k]]) for k in (0, 2)])
    sent = jnp.stack([jnp.concatenate([pre[k].astype(BF16), back[k].astype(BF16)]) for k in (1, 3)])
    gate_pre, up_pre, hidden_grad = scatter(kept, sent, "x", their_near)
    sig = jax.nn.sigmoid(gate_pre)
    hidden = (gate_pre * sig * up_pre).astype(BF16)
    gate_grad = (hidden_grad * up_pre * sig * (1.0 + gate_pre * (1.0 - sig))).astype(BF16)
    up_grad = (hidden_grad * gate_pre * sig).astype(BF16)
    own_acts = jnp.stack([hidden, gate_grad, up_grad])

    pair, far = gather(own_acts, "x", jnp.stack)
    their_acts = swap(own_acts, "dp")
    far = after(far, their_acts)
    acts = (pair, far, swap(pair, "core"), swap(far, "core"))
    their_rest = exchange(jnp.concatenate([their_z, their_near], axis=0), "y", 1)

    kept, sent = outputs(core, block_mask, acts, w_gate, w_up, w_down)
    their_pair = jnp.stack([their_acts, exchange(after(their_acts, far), "x", 0)])
    own = own_grads(core, block_mask, tokens, cots, acts)
    their_far = exchange(their_pair, "x", 1)
    both = kept + exchange(after(sent, their_rest), "y", 0).astype(F32)
    second = exchange(after(both[1].astype(BF16), own[0], their_pair), "y", 1)
    total = both[0] + second.astype(F32)

    total = after(total, their_far)
    total = jnp.concatenate(
        [lax.dot_general(pick, side, COLS, precision="highest", preferred_element_type=F32) for side in total], axis=1
    ).reshape(4, rows, 2 * feats)
    theirs = (their_z, their_near, their_rest)
    their_acts = (their_pair, their_far, swap(their_pair, "core"), swap(their_far, "core"))
    grads = all_grads(core, block_mask, theirs, their_acts, own)
    sent = total[1:].astype(BF16)
    total = total[0] + (
        exchange(sent[0], "zh", 0).astype(F32)
        + exchange(sent[1], "zh", 1).astype(F32)
        + across(sent[2], "zh").astype(F32)
    )
    total = total.astype(BF16)
    return total[:, :feats], total[:, feats:], *grads


def solution(mesh):
    split = Mesh(mesh.devices.reshape(2, 4, 4, 4, 2), ("dp", "y", "zh", "x", "core"))
    token_rows = P(("dp", "y", "zh"), ("x", "core"))
    weight_in = P(("x", "core"), ("y", "zh"))
    weight_out = P(("y", "zh"), ("x", "core"))
    return jax.shard_map(
        local,
        mesh=split,
        in_specs=(token_rows, token_rows, weight_in, weight_in, weight_out, weight_in),
        out_specs=(token_rows, token_rows, weight_in, weight_in, weight_out),
        check_vma=False,
    )
```
